32 devices in a mesh: row: 4 (over y, x), col: 8 (over z, core).
Axes of the slice: x: 2, y: 2, z: 4, core: 2. Of those that a mesh axis runs over, the one named last changes fastest.
Arguments:
- tiles: bfloat16 [256, 256, 256], P(('row', 'col')), may hold values from -0.09375 to 0.09375
- tile_rows: int32 [256], P(('row', 'col')), may hold values from 0 to 3, as said below
- tile_cols: int32 [256], P(('row', 'col')), may hold values from 0 to 1
- tile_count: int32 [32], P(('row', 'col')), may hold values from 0 to 8, as said below
- bounds: float32 [2], replicated, may hold values from -1 to 2, as said below
- vectors: float32 [4096, 128], P(('row', 'col')), may hold values from -6 to 6
Outputs:
- filtered: float32 [4096, 128], P(('row', 'col'))
- gram: float32 [128, 128], replicated
The draws below stay inside these ranges and needn't reach their ends.
Inputs may be any that keep to these rules, and one draw needn't show every extreme that they name: `tile_rows`: within each device the first tile_count slots name distinct blocks with global block row I <= global block column J; the device's diagonal blocks (I = J) come first; every diagonal block of the Hamiltonian is stored; slots after the live ones hold valid indices but are not part of the matrix. `tile_count`: devices whose block rows all lie below their block columns have no live slot; some device has all 8 slots live. bounds[0] < -0.5 and bounds[1] > 1.0.
All inputs are finite; a program needn't handle non-finite values.
Results may differ from the reference program's by a relative error of at most 0.0037.
Values may be sent and summed in bfloat16 or wider, within the bound.
A program may use at most 64 MiB of HBM per device.

```python
import jax
import jax.numpy as jnp
from jax import lax

BS = 256
K = 128
BLK_COL = 2
DEGREE = 2
TILES_DEV = 8
TILES = 256
NB = 16
N = 4096
N_ROW = 4
N_COL = 8
DEVICES = 32


def pattern_tables(key):
    col_ratio = N_COL // N_ROW
    row_blocks = BLK_COL * col_ratio
    device = jnp.arange(DEVICES, dtype=jnp.int32)
    row_index = device // N_COL
    col_index = device % N_COL
    slots = jnp.arange(TILES_DEV, dtype=jnp.int32)
    local_row = slots // BLK_COL
    local_col = slots % BLK_COL
    global_row = row_index[:, None] * row_blocks + local_row[None, :]
    global_col = col_index[:, None] * BLK_COL + local_col[None, :]
    allowed = global_row <= global_col
    diagonal = global_row == global_col
    noise = jax.random.randint(jax.random.fold_in(key, 11), (DEVICES, TILES_DEV), 0, 65536)
    score = jnp.where(diagonal, 0, jnp.where(allowed, 1 + noise, 131072))
    score = score * TILES_DEV + slots[None, :]
    order = jnp.argsort(score, axis=1, stable=True)
    rows_full = jnp.broadcast_to(local_row[None, :], (DEVICES, TILES_DEV))
    cols_full = jnp.broadcast_to(local_col[None, :], (DEVICES, TILES_DEV))
    rows_out = jnp.take_along_axis(rows_full, order, axis=1)
    cols_out = jnp.take_along_axis(cols_full, order, axis=1)
    allowed_count = jnp.sum(allowed.astype(jnp.int32), axis=1)
    diagonal_count = jnp.sum(diagonal.astype(jnp.int32), axis=1)
    drawn = jax.random.randint(jax.random.fold_in(key, 12), (DEVICES,), 1, TILES_DEV + 1)
    counts = jnp.minimum(jnp.maximum(drawn, diagonal_count), allowed_count)
    counts = jnp.where(device == N_COL - 1, TILES_DEV, counts)
    return (rows_out.reshape(-1).astype(jnp.int32), cols_out.reshape(-1).astype(jnp.int32), counts.astype(jnp.int32))


def draw_tile_rows(key, part):
    return pattern_tables(key)[0]


def draw_tile_cols(key, part):
    return pattern_tables(key)[1]


def draw_tile_count(key, part):
    return pattern_tables(key)[2]


def draw_bounds(key, part):
    unit = jax.random.uniform(key, (2,), jnp.float32)
    lower = -1.0 + 0.45 * unit[0]
    upper = 1.05 + 0.9 * unit[1]
    return jnp.stack([lower, upper]).astype(jnp.float32)


def level_of(stream_key, dims, cuts, low, top_value):
    def one(axis_at, blocks):
        heights = jax.random.uniform(jax.random.fold_in(jax.random.fold_in(stream_key, 6), axis_at), (blocks,), jnp.float32, low / len(cuts), top_value / len(cuts))
        return jnp.repeat(jnp.exp(heights), dims[axis_at] // blocks).reshape((-1,) + (1,) * (len(dims) - axis_at - 1))

    gain = one(*cuts[0])
    for cut in cuts[1:]:
        gain = gain * one(*cut)
    return gain


def bell_draw(stream_key, shape, width, bound, split=(), kind=jnp.bfloat16):
    result = jax.random.normal(stream_key, shape, jnp.float32) * width
    if len(split) > 0:
        result = level_of(stream_key, shape, split, -0.22, 0.18) * result
    return jnp.clip(result, min=-bound, max=bound).astype(kind)


def setup_inputs(seed: int = 0) -> dict:
    key_of = jax.random.split(jax.random.key(seed), 7)
    tiles = bell_draw(key_of[0], (TILES, BS, BS), N ** -0.5, 0.09375, ((0, 32),))
    tile_rows = draw_tile_rows(jax.random.fold_in(key_of[6], 71), 0)
    tile_cols = draw_tile_cols(jax.random.fold_in(key_of[6], 71), 0)
    tile_count = draw_tile_count(jax.random.fold_in(key_of[6], 71), 0)
    bounds = draw_bounds(jax.random.fold_in(key_of[6], 71), 0)
    vectors = bell_draw(key_of[5], (N, K), 1.0, 6.0, ((0, 32),), jnp.float32)
    return dict(tiles=tiles, tile_rows=tile_rows, tile_cols=tile_cols, tile_count=tile_count, bounds=bounds, vectors=vectors)


def apply_hamiltonian(current, tiles, global_row, global_col, live_mask):
    blocks = current.astype(jnp.bfloat16).reshape(NB, BS, K)
    steps = tiles.shape[0] // TILES_DEV

    def add_device(total, device):
        start = device * TILES_DEV
        some_tiles = lax.dynamic_slice_in_dim(tiles, start, TILES_DEV, 0).astype(jnp.float32)
        rows_here = lax.dynamic_slice_in_dim(global_row, start, TILES_DEV, 0)
        cols_here = lax.dynamic_slice_in_dim(global_col, start, TILES_DEV, 0)
        mask_here = lax.dynamic_slice_in_dim(live_mask, start, TILES_DEV, 0)
        col_input = blocks[cols_here].astype(jnp.float32)
        row_input = blocks[rows_here].astype(jnp.float32)
        forward = jnp.einsum('tab,tbk->tak', some_tiles, col_input)
        backward = jnp.einsum('tab,tak->tbk', some_tiles, row_input)
        forward = jnp.where(mask_here[:, None, None], forward, jnp.float32(0.0))
        backward = jnp.where(mask_here[:, None, None], backward, jnp.float32(0.0))
        total = total.at[rows_here].add(forward)
        total = total.at[cols_here].add(backward)
        return total, None

    start_total = jnp.zeros((NB, BS, K), jnp.float32)
    total, _ = lax.scan(add_device, start_total, jnp.arange(steps, dtype=jnp.int32))
    return total.reshape(N, K)


def reference(tiles, tile_rows, tile_cols, tile_count, bounds, vectors):
    col_ratio = N_COL // N_ROW
    row_blocks = BLK_COL * col_ratio
    slot_ids = jnp.arange(TILES, dtype=jnp.int32)
    device = slot_ids // TILES_DEV
    global_row = ((device // N_COL) * row_blocks + tile_rows).astype(jnp.int32)
    global_col = ((device % N_COL) * BLK_COL + tile_cols).astype(jnp.int32)
    live_mask = (slot_ids % TILES_DEV) < tile_count[device]
    center = (bounds[1] + bounds[0]) * 0.5
    halfwidth = (bounds[1] - bounds[0]) * 0.5
    previous = vectors
    current = (apply_hamiltonian(vectors, tiles, global_row, global_col, live_mask) - center * vectors) / halfwidth
    for degree_step in range(DEGREE - 1):
        image = apply_hamiltonian(current, tiles, global_row, global_col, live_mask)
        following = 2.0 * (image - center * current) / halfwidth - previous
        previous = current
        current = following
    gram = jnp.dot(current.T, current, precision=lax.Precision.HIGHEST, preferred_element_type=jnp.float32) / N
    return current, gram
```

```python
import functools

import jax
import jax.numpy as jnp
from jax import lax
from jax.experimental import pallas as pl
from jax.experimental.pallas import tpu as pltpu
from jax.sharding import PartitionSpec as P

BLK_COL = 2
GRAM_ROWS = 8
MESH = pl.DeviceIdType.MESH


def body(
    n_row,
    n_col,
    tile_rows,
    tile_cols,
    tile_count,
    bounds,
    tiles_hbm,
    vectors,
    filtered,
    gram,
    tiles,
    panel_h,
    panel_t,
    piece,
    panel,
    fwd,
    bwd,
    fwd_send,
    bwd_send,
    landed,
    current,
    gram_part,
    gram_land,
    gram_sum,
    gram_all,
    tile_sem,
    ga_send,
    ga_recv,
    sc_send,
    sc_recv,
    gram_sems,
):
    slots, size, _ = tiles_hbm.shape
    share, width = vectors.shape
    ratio = n_col // n_row
    group = share * n_col
    blocks = group // size
    column = BLK_COL * size
    owners = column // share
    n_dev = n_row * n_col
    reducers = width // GRAM_ROWS
    stride = n_dev // reducers
    row, col = lax.axis_index("row"), lax.axis_index("col")
    me = row * n_col + col
    live = row * ratio <= col
    diagonal = row == col // ratio
    first_live = row * ratio
    column_of_mine = row * ratio + col // owners
    place_in_column = col % owners
    column_base = jnp.where(diagonal, (col % ratio) * owners, n_col)

    def loop(low, high, step):
        def run(i, carry):
            step(i)
            return carry

        lax.fori_loop(low, high, run, 0)

    def device(index):
        return (index // n_col, index % n_col)

    tile_copy = pltpu.make_async_copy(tiles_hbm, tiles.at[pl.ds(0, slots)], tile_sem)
    tile_copy.start()

    barrier = pltpu.get_barrier_semaphore()

    def greet(i):
        pl.semaphore_signal(
            barrier, inc=1, device_id=device(lax.rem(me + i, n_dev)), device_id_type=MESH
        )

    loop(1, n_dev, greet)

    center = (bounds[1] + bounds[0]) * 0.5
    halfwidth = (bounds[1] - bounds[0]) * 0.5
    piece[0] = vectors[...].astype(jnp.bfloat16)
    tiles[slots] = jnp.zeros((size, size), jnp.bfloat16)
    pl.semaphore_wait(barrier, n_dev - 1)

    def gather_row(k, other):
        return pltpu.make_async_remote_copy(
            src_ref=piece.at[k],
            dst_ref=panel.at[k, col],
            send_sem=ga_send.at[k, other],
            recv_sem=ga_recv.at[k, col],
            device_id=(row, other),
            device_id_type=MESH,
        )

    def gather_column(k, other):
        return pltpu.make_async_remote_copy(
            src_ref=piece.at[k],
            dst_ref=panel.at[k, n_col + place_in_column],
            send_sem=ga_send.at[k, n_col + other],
            recv_sem=ga_recv.at[k, n_col + place_in_column],
            device_id=(other, column_of_mine),
            device_id_type=MESH,
        )

    def gather_landed(k, slot):
        return pltpu.make_async_remote_copy(
            src_ref=piece.at[k],
            dst_ref=panel.at[k, slot],
            send_sem=ga_send.at[k, 0],
            recv_sem=ga_recv.at[k, slot],
            device_id=(row, lax.rem(col + 1, n_col)),
            device_id_type=MESH,
        )

    def scatter_row(k, other):
        return pltpu.make_async_remote_copy(
            src_ref=fwd_send.at[k, other],
            dst_ref=landed.at[k, col],
            send_sem=sc_send.at[k, other],
            recv_sem=sc_recv.at[k, col],
            device_id=(row, other),
            device_id_type=MESH,
        )

    def scatter_column(k, j):
        return pltpu.make_async_remote_copy(
            src_ref=bwd_send.at[k, j],
            dst_ref=landed.at[k, n_col + row],
            send_sem=sc_send.at[k, n_col + j],
            recv_sem=sc_recv.at[k, n_col + row],
            device_id=(col // ratio, (col % ratio) * owners + j),
            device_id_type=MESH,
        )

    def scatter_landed(k, slot):
        return pltpu.make_async_remote_copy(
            src_ref=piece.at[k],
            dst_ref=landed.at[k, slot],
            send_sem=sc_send.at[k, 0],
            recv_sem=sc_recv.at[k, slot],
            device_id=(row, lax.rem(col + 1, n_col)),
            device_id_type=MESH,
        )

    def not_me(other, action):
        @pl.when(other != col)
        def _():
            action()

    def start_gather(k):
        loop(first_live, n_col, lambda i: not_me(i, lambda: gather_row(k, i).start()))
        loop(0, row, lambda i: gather_column(k, i).start())

    def arrange():
        tile_copy.wait()
        for i in range(blocks):
            for j in range(BLK_COL):
                slot = jnp.int32(slots)
                for s in range(slots):
                    here = (tile_rows[s] == i) & (tile_cols[s] == j) & (s < tile_count[0])
                    slot = jnp.where(here, jnp.int32(s), slot)
                block = tiles[slot]
                panel_h[pl.ds(i * size, size), pl.ds(j * size, size)] = block
                panel_t[pl.ds(j * size, size), pl.ds(i * size, size)] = block.T

    def products(k):
        panel[k, col] = piece[k]
        loop(0, n_col, lambda i: not_me(i, lambda: gather_landed(k, i).wait_recv()))

        @pl.when(jnp.logical_not(diagonal))
        def _():
            loop(0, owners, lambda j: gather_landed(k, n_col + j).wait_recv())

        rows_in = panel[k, pl.ds(0, n_col)].reshape(group, width)
        cols_in = panel[k, pl.ds(column_base, owners)].reshape(column, width)
        for j in range(BLK_COL):
            part = jnp.dot(
                panel_t[pl.ds(j * size, size)], rows_in, preferred_element_type=jnp.float32
            )
            bwd[pl.ds(j * size, size)] = part
        for i in range(blocks):
            part = jnp.dot(
                panel_h[pl.ds(i * size, size)], cols_in, preferred_element_type=jnp.float32
            )
            fwd[pl.ds(i * size, size)] = part

        @pl.when(diagonal)
        def _():
            here = pl.ds(pl.multiple_of((col % ratio) * column, column), column)
            fwd[here] += bwd[...]

        fwd_send[k] = fwd[...].astype(jnp.bfloat16).reshape(n_col, share, width)
        loop(0, n_col, lambda i: not_me(i, lambda: scatter_row(k, i).start()))

        @pl.when(jnp.logical_not(diagonal))
        def _():
            bwd_send[k] = bwd[...].astype(jnp.bfloat16).reshape(owners, share, width)
            loop(0, owners, lambda j: scatter_column(k, j).start())

    def apply(k):
        @pl.when(live)
        def _():
            if k == 0:
                arrange()
            products(k)

        if k == 0:

            @pl.when(jnp.logical_not(live))
            def _():
                tile_copy.wait()

        @pl.when(live)
        def _():
            filtered[...] = fwd[pl.ds(pl.multiple_of(col * share, share), share)]

        @pl.when(jnp.logical_not(live))
        def _():
            filtered[...] = jnp.zeros_like(filtered)

        def add(slot):
            scatter_landed(k, slot).wait_recv()
            filtered[...] += landed[k, slot].astype(jnp.float32)

        loop(first_live, n_col, lambda i: not_me(i, lambda: add(i)))
        loop(0, row, lambda i: add(n_col + i))
        return filtered[...]

    def finish_sends(k):
        loop(first_live, n_col, lambda i: not_me(i, lambda: gather_row(k, i).wait_send()))
        loop(0, row, lambda i: gather_column(k, i).wait_send())

        @pl.when(live)
        def _():
            loop(0, n_col, lambda i: not_me(i, lambda: scatter_row(k, i).wait_send()))

            @pl.when(jnp.logical_not(diagonal))
            def _():
                loop(0, owners, lambda j: scatter_column(k, j).wait_send())

    start_gather(0)
    image = apply(0)
    first = (image - center * vectors[...]) / halfwidth
    current[...] = first
    piece[1] = first.astype(jnp.bfloat16)
    start_gather(1)
    image = apply(1)
    last = 2.0 * (image - center * current[...]) / halfwidth - vectors[...]
    filtered[...] = last

    part = lax.dot_general(
        last,
        last,
        (((0,), (0,)), ((), ())),
        precision=lax.Precision.HIGHEST,
        preferred_element_type=jnp.float32,
    )
    gram_part[...] = part.reshape(reducers, GRAM_ROWS, width)
    reduces = lax.rem(me, stride) == 0
    mine = me // stride

    def to_reducer(q):
        target = q * stride
        return pltpu.make_async_remote_copy(
            src_ref=gram_part.at[q],
            dst_ref=gram_land.at[lax.rem(me - target - 1 + n_dev, n_dev)],
            send_sem=gram_sems.at[0],
            recv_sem=gram_sems.at[1],
            device_id=device(target),
            device_id_type=MESH,
        )

    def from_reducer(i):
        return pltpu.make_async_remote_copy(
            src_ref=gram_sum,
            dst_ref=gram_all.at[mine],
            send_sem=gram_sems.at[2],
            recv_sem=gram_sems.at[3],
            device_id=device(lax.rem(me + i, n_dev)),
            device_id_type=MESH,
        )

    def wait_bytes(ref, sem):
        pltpu.make_async_copy(ref, ref, gram_sems.at[sem]).wait()

    def start_reduce(q):
        @pl.when(q * stride != me)
        def _():
            to_reducer(q).start()

    loop(0, reducers, start_reduce)
    finish_sends(0)

    @pl.when(reduces)
    def _():
        wait_bytes(gram_land, 1)
        total = gram_part[mine] + jnp.sum(gram_land[...], axis=0)
        gram_sum[...] = total / (share * n_dev)
        gram_all[mine] = gram_sum[...]
        loop(1, n_dev, lambda i: from_reducer(i).start())

    finish_sends(1)

    @pl.when(reduces)
    def _():
        wait_bytes(gram_part.at[pl.ds(0, reducers - 1)], 0)
        wait_bytes(gram_all.at[pl.ds(0, reducers - 1)], 3)
        wait_bytes(gram_land, 2)

    @pl.when(jnp.logical_not(reduces))
    def _():
        wait_bytes(gram_part, 0)
        wait_bytes(gram_all, 3)

    gram[...] = gram_all[...].reshape(width, width)


def on_device(n_row, n_col, tiles, tile_rows, tile_cols, tile_count, bounds, vectors):
    slots, size, _ = tiles.shape
    share, width = vectors.shape
    group = share * n_col
    column = BLK_COL * size
    owners = column // share
    reducers = width // GRAM_ROWS
    n_dev = n_row * n_col
    smem = pl.BlockSpec(memory_space=pltpu.SMEM)
    vmem = pl.BlockSpec(memory_space=pltpu.VMEM)
    half, full = jnp.bfloat16, jnp.float32
    return pl.pallas_call(
        functools.partial(body, n_row, n_col),
        out_shape=(
            jax.ShapeDtypeStruct((share, width), full),
            jax.ShapeDtypeStruct((width, width), full),
        ),
        in_specs=[smem, smem, smem, smem, pl.BlockSpec(memory_space=pl.ANY), vmem],
        out_specs=(vmem, vmem),
        scratch_shapes=[
            pltpu.VMEM((slots + 1, size, size), half),
            pltpu.VMEM((group, column), half),
            pltpu.VMEM((column, group), half),
            pltpu.VMEM((2, share, width), half),
            pltpu.VMEM((2, n_col + owners, share, width), half),
            pltpu.VMEM((group, width), full),
            pltpu.VMEM((column, width), full),
            pltpu.VMEM((2, n_col, share, width), half),
            pltpu.VMEM((2, owners, share, width), half),
            pltpu.VMEM((2, n_col + n_row, share, width), half),
            pltpu.VMEM((share, width), full),
            pltpu.VMEM((reducers, GRAM_ROWS, width), full),
            pltpu.VMEM((n_dev - 1, GRAM_ROWS, width), full),
            pltpu.VMEM((GRAM_ROWS, width), full),
            pltpu.VMEM((reducers, GRAM_ROWS, width), full),
            pltpu.SemaphoreType.DMA(()),
            pltpu.SemaphoreType.DMA((2, n_col + n_row)),
            pltpu.SemaphoreType.DMA((2, n_col + owners)),
            pltpu.SemaphoreType.DMA((2, n_col + owners)),
            pltpu.SemaphoreType.DMA((2, n_col + n_row)),
            pltpu.SemaphoreType.DMA((4,)),
        ],
        compiler_params=pltpu.CompilerParams(
            collective_id=0, has_side_effects=True, vmem_limit_bytes=48 * 1024 * 1024
        ),
    )(tile_rows, tile_cols, tile_count, bounds, tiles, vectors)


def solution(mesh):
    in_specs = (
        P(("row", "col"), None, None),
        P(("row", "col")),
        P(("row", "col")),
        P(("row", "col")),
        P(),
        P(("row", "col"), None),
    )
    out_specs = (P(("row", "col"), None), P())
    return jax.shard_map(
        functools.partial(on_device, mesh.shape["row"], mesh.shape["col"]),
        mesh=mesh,
        in_specs=in_specs,
        out_specs=out_specs,
        check_vma=False,
    )
```

```python
import functools

import jax
import jax.numpy as jnp
from jax import lax
from jax.experimental import pallas as pl
from jax.experimental.pallas import tpu as pltpu
from jax.sharding import PartitionSpec as P

BLK_COL = 2
UNROLL = 8
MESH = pl.DeviceIdType.MESH


def body(
    n_row,
    n_col,
    rows_any,
    cols_any,
    count_any,
    bounds_any,
    tiles_any,
    vectors_any,
    filtered,
    gram,
    tile_rows,
    tile_cols,
    tile_count,
    bounds,
    tiles,
    vectors,
    panel_h,
    panel_t,
    piece,
    panel,
    fwd,
    bwd,
    swapped,
    fwd_send,
    bwd_send,
    landed,
    current,
    gram_part,
    gram_half,
    gram_z,
    gram_xy,
    in_sems,
    ga_send,
    ga_recv,
    swap_sems,
    sc_send,
    sc_recv,
    gram_sems,
):
    slots, size, _ = tiles_any.shape
    share, width = vectors.shape
    n_z = n_col // 2
    ratio = n_col // n_row
    group = share * n_col
    blocks = group // size
    column = BLK_COL * size
    owners = column // share
    pairs = size // (2 * share)
    n_dev = n_row * n_col
    row, col = lax.axis_index("row"), lax.axis_index("col")
    core = lax.rem(col, 2)
    zed = col // 2
    sibling = zed * 2 + 1 - core
    live = row * ratio <= col
    diagonal = row == col // ratio
    first_z = row * ratio // 2
    column_of_mine = row * ratio + col // owners
    place_in_column = lax.rem(col, owners)
    part_of_column = lax.rem(col, ratio)
    column_base = jnp.where(diagonal, part_of_column * owners, n_col)

    def loop(count, step):
        def run(i, carry):
            step(i)
            return carry

        if count <= UNROLL:
            for i in range(count):
                step(i)
        else:
            lax.fori_loop(0, count, run, 0)

    def when(condition, action):
        pl.when(condition)(action)

    def far_first(i):
        return jnp.where(zed < n_z // 2, n_z - 1 - i, i)

    def near_first(i):
        return jnp.where(zed < n_z // 2, i, n_z - 1 - i)

    def when_not(value, mine, action):
        @pl.when(value != mine)
        def _():
            action()

    inputs = [
        pltpu.make_async_copy(vectors_any, vectors, in_sems.at[0]),
        pltpu.make_async_copy(tiles_any, tiles.at[pl.ds(0, slots)], in_sems.at[1]),
        pltpu.make_async_copy(rows_any, tile_rows, in_sems.at[2]),
        pltpu.make_async_copy(cols_any, tile_cols, in_sems.at[3]),
        pltpu.make_async_copy(count_any, tile_count, in_sems.at[4]),
        pltpu.make_async_copy(bounds_any, bounds, in_sems.at[5]),
    ]
    for copy in inputs:
        copy.start()

    barrier = pltpu.get_barrier_semaphore()

    def greet(other_row, other_col):
        pl.semaphore_signal(
            barrier, inc=1, device_id=(other_row, other_col), device_id_type=MESH
        )

    greet(row, sibling)
    loop(n_z, lambda z: when_not(z, zed, lambda: greet(row, z * 2 + core)))
    loop(n_row, lambda i: when_not(i, row, lambda: greet(i, col)))
    loop(n_row, lambda i: when_not(i, row, lambda: greet(i, sibling)))
    loop(n_row, lambda i: when(i < row, lambda: greet(i, column_of_mine)))
    across = live & jnp.logical_not(diagonal)

    @pl.when(across)
    def _():
        loop(owners, lambda j: greet(col // ratio, part_of_column * owners + j))

    inputs[0].wait()
    piece[0] = vectors[...].astype(jnp.bfloat16)
    tiles[slots] = jnp.zeros((size, size), jnp.bfloat16)
    pl.semaphore_wait(
        barrier, n_z + 2 * (n_row - 1) + row + jnp.where(across, owners, 0)
    )

    def remote(src, dst, send, recv, other_row, other_col):
        return pltpu.make_async_remote_copy(
            src_ref=src,
            dst_ref=dst,
            send_sem=send,
            recv_sem=recv,
            device_id=(other_row, other_col),
            device_id_type=MESH,
        )

    def gather_row(k, z):
        other = z * 2 + core
        return remote(
            piece.at[k], panel.at[k, col], ga_send.at[k, other], ga_recv.at[k, col], row, other
        )

    def gather_pair(k, z):
        slot = z * 2 + core
        return remote(
            panel.at[k, slot],
            panel.at[k, slot],
            ga_send.at[k, z * 2 + 1 - core],
            ga_recv.at[k, slot],
            row,
            sibling,
        )

    def gather_column(k, other):
        slot = n_col + place_in_column
        return remote(
            piece.at[k],
            panel.at[k, slot],
            ga_send.at[k, n_col + other],
            ga_recv.at[k, slot],
            other,
            column_of_mine,
        )

    def gather_landed(k, slot):
        return remote(
            piece.at[k], panel.at[k, slot], ga_send.at[k, 0], ga_recv.at[k, slot], row, sibling
        )

    def swap(k, z):
        return remote(
            fwd.at[1 - core, z],
            swapped.at[k, z],
            swap_sems.at[k, 0, z],
            swap_sems.at[k, 1, z],
            row,
            sibling,
        )

    def scatter_row(k, z):
        return remote(
            fwd_send.at[k, z],
            landed.at[k, zed],
            sc_send.at[k, z],
            sc_recv.at[k, zed],
            row,
            z * 2 + core,
        )

    def scatter_column(k, j):
        return remote(
            bwd_send.at[k, lax.rem(j, 2), j // 2],
            landed.at[k, n_z + row],
            sc_send.at[k, n_z + j],
            sc_recv.at[k, n_z + row],
            col // ratio,
            part_of_column * owners + j,
        )

    def scatter_landed(k, slot):
        return remote(
            piece.at[k], landed.at[k, slot], sc_send.at[k, 0], sc_recv.at[k, slot], row, sibling
        )

    def start_gather(k):
        @pl.when(live)
        def _():
            panel[k, col] = piece[k]

        def to_row(i):
            z = far_first(i)
            when((z >= first_z) & (z != zed), lambda: gather_row(k, z).start())

        loop(n_z, to_row)
        loop(n_row, lambda i: when(i < row, lambda: gather_column(k, i).start()))
        when(live, lambda: gather_pair(k, zed).start())

    def arrange():
        for i in range(blocks):
            for j in range(BLK_COL):
                slot = jnp.int32(slots)
                for s in range(slots):
                    here = (tile_rows[s] == i) & (tile_cols[s] == j) & (s < tile_count[0])
                    slot = jnp.where(here, jnp.int32(s), slot)
                block = tiles[slot]
                panel_h[pl.ds(i * size, size), pl.ds(j * size, size)] = block
                panel_t[pl.ds(j * size, size), pl.ds(i * size, size)] = block.T

    def forward_pair(k, z):
        gather_landed(k, z * 2 + core).wait_recv()
        gather_pair(k, z).start()

    def backward(k):
        rows_in = panel[k, pl.ds(0, n_col)].reshape(group, width)
        for j in range(BLK_COL):
            part = jnp.dot(
                panel_t[pl.ds(j * size, size)], rows_in, preferred_element_type=jnp.float32
            ).reshape(pairs, 2, share, width)
            for half in range(2):
                bwd[half, pl.ds(j * pairs, pairs)] = part[:, half]

    def products(k):
        def forward(i):
            z = near_first(i)
            when_not(z, zed, lambda: forward_pair(k, z))

        def rest_of_row():
            loop(n_z, lambda z: gather_landed(k, z * 2 + 1 - core).wait_recv())

        loop(n_z, forward)

        @pl.when(across)
        def _():
            loop(owners, lambda j: gather_landed(k, n_col + j).wait_recv())

        @pl.when(diagonal)
        def _():
            rest_of_row()
            backward(k)

        cols_in = panel[k, pl.ds(column_base, owners)].reshape(column, width)
        for i in range(blocks):
            part = jnp.dot(
                panel_h[pl.ds(i * size, size)], cols_in, preferred_element_type=jnp.float32
            ).reshape(pairs, 2, share, width)
            for half in range(2):
                fwd[half, pl.ds(i * pairs, pairs)] = part[:, half]

        @pl.when(diagonal)
        def _():
            here = pl.ds(part_of_column * (owners // 2), owners // 2)
            for half in range(2):
                fwd[half, here] += bwd[half]

        loop(n_z, lambda i: swap(k, far_first(i)).start())

        @pl.when(across)
        def _():
            rest_of_row()
            backward(k)
            bwd_send[k] = bwd[...].astype(jnp.bfloat16)
            loop(owners, lambda j: scatter_column(k, j).start())

        def send(i):
            z = far_first(i)
            swap(k, z).wait_recv()

            @pl.when(z != zed)
            def _():
                fwd_send[k, z] = (fwd[core, z] + swapped[k, z]).astype(jnp.bfloat16)
                scatter_row(k, z).start()

        loop(n_z, send)
        filtered[...] = fwd[core, zed] + swapped[k, zed]
        loop(n_z, lambda z: swap(k, z).wait_send())

    def apply(k):
        if k == 0:
            for copy in inputs[1:]:
                copy.wait()

        @pl.when(live)
        def _():
            if k == 0:
                arrange()
            products(k)

        @pl.when(jnp.logical_not(live))
        def _():
            filtered[...] = jnp.zeros_like(filtered)

        def add(slot):
            scatter_landed(k, slot).wait_recv()
            filtered[...] += landed[k, slot].astype(jnp.float32)

        def add_row(i):
            z = near_first(i)
            when((z >= first_z) & (z != zed), lambda: add(z))

        loop(n_z, add_row)
        loop(n_row, lambda i: when(i < row, lambda: add(n_z + i)))
        return filtered[...]

    def finish_sends(k):
        def sent(z):
            when((z >= first_z) & (z != zed), lambda: gather_row(k, z).wait_send())

        loop(n_z, sent)
        loop(n_row, lambda i: when(i < row, lambda: gather_column(k, i).wait_send()))

        @pl.when(live)
        def _():
            loop(n_z, lambda z: gather_pair(k, z).wait_send())
            loop(n_z, lambda z: when_not(z, zed, lambda: scatter_row(k, z).wait_send()))

        @pl.when(across)
        def _():
            loop(owners, lambda j: scatter_column(k, j).wait_send())

    start_gather(0)
    image = apply(0)
    center = (bounds[1] + bounds[0]) * 0.5
    halfwidth = (bounds[1] - bounds[0]) * 0.5
    first = (image - center * vectors[...]) / halfwidth
    current[...] = first
    piece[1] = first.astype(jnp.bfloat16)
    start_gather(1)
    image = apply(1)
    last = 2.0 * (image - center * current[...]) / halfwidth - vectors[...]
    filtered[...] = last

    part = lax.dot_general(
        last,
        last,
        (((0,), (0,)), ((), ())),
        precision=lax.Precision.HIGHEST,
        preferred_element_type=jnp.float32,
    )
    height = width // 2
    gram_part[...] = part.reshape(2, height, width)

    def gram_swap():
        return remote(
            gram_part.at[1 - core], gram_half, gram_sems.at[0], gram_sems.at[1], row, sibling
        )

    def gram_row(z):
        return remote(
            gram_z.at[zed],
            gram_z.at[zed],
            gram_sems.at[2],
            gram_sems.at[3],
            row,
            z * 2 + core,
        )

    def gram_out(i, other):
        here = core * n_row + row
        return remote(
            gram_xy.at[here], gram_xy.at[here], gram_sems.at[4], gram_sems.at[5], i, other
        )

    def wait_bytes(ref, sem):
        pltpu.make_async_copy(ref, ref, gram_sems.at[sem]).wait()

    gram_swap().start()
    finish_sends(0)
    gram_swap().wait_recv()
    gram_z[zed] = gram_part[core] + gram_half[...]

    def to_row(i):
        z = far_first(i)
        when_not(z, zed, lambda: gram_row(z).start())

    loop(n_z, to_row)
    finish_sends(1)
    gram_swap().wait_send()
    wait_bytes(gram_z.at[pl.ds(0, n_z - 1)], 3)
    gram_xy[core * n_row + row] = jnp.sum(gram_z[...], axis=0)
    loop(n_row, lambda i: when_not(i, row, lambda: gram_out(i, col).start()))
    loop(n_row, lambda i: when_not(i, row, lambda: gram_out(i, sibling).start()))
    gram_out(row, sibling).start()
    wait_bytes(gram_z.at[pl.ds(0, n_z - 1)], 2)
    wait_bytes(gram_xy.at[pl.ds(0, 2 * n_row - 1)], 5)
    for half in range(2):
        total = jnp.sum(gram_xy[pl.ds(half * n_row, n_row)], axis=0)
        gram[pl.ds(half * height, height)] = total / (share * n_dev)
    wait_bytes(gram_xy.at[pl.ds(0, 2 * n_row - 1)], 4)


def on_device(n_row, n_col, tiles, tile_rows, tile_cols, tile_count, bounds, vectors):
    slots, size, _ = tiles.shape
    share, width = vectors.shape
    n_z = n_col // 2
    group = share * n_col
    column = BLK_COL * size
    owners = column // share
    height = width // 2
    hbm = pl.BlockSpec(memory_space=pl.ANY)
    vmem = pl.BlockSpec(memory_space=pltpu.VMEM)
    half, full = jnp.bfloat16, jnp.float32
    return pl.pallas_call(
        functools.partial(body, n_row, n_col),
        out_shape=(
            jax.ShapeDtypeStruct((share, width), full),
            jax.ShapeDtypeStruct((width, width), full),
        ),
        in_specs=[hbm] * 6,
        out_specs=(vmem, vmem),
        scratch_shapes=[
            pltpu.SMEM((slots,), jnp.int32),
            pltpu.SMEM((slots,), jnp.int32),
            pltpu.SMEM((1,), jnp.int32),
            pltpu.SMEM((2,), full),
            pltpu.VMEM((slots + 1, size, size), half),
            pltpu.VMEM((share, width), full),
            pltpu.VMEM((group, column), half),
            pltpu.VMEM((column, group), half),
            pltpu.VMEM((2, share, width), half),
            pltpu.VMEM((2, n_col + owners, share, width), half),
            pltpu.VMEM((2, n_z, share, width), full),
            pltpu.VMEM((2, owners // 2, share, width), full),
            pltpu.VMEM((2, n_z, share, width), full),
            pltpu.VMEM((2, n_z, share, width), half),
            pltpu.VMEM((2, 2, owners // 2, share, width), half),
            pltpu.VMEM((2, n_z + n_row, share, width), half),
            pltpu.VMEM((share, width), full),
            pltpu.VMEM((2, height, width), full),
            pltpu.VMEM((height, width), full),
            pltpu.VMEM((n_z, height, width), full),
            pltpu.VMEM((2 * n_row, height, width), full),
            pltpu.SemaphoreType.DMA((6,)),
            pltpu.SemaphoreType.DMA((2, n_col + n_row)),
            pltpu.SemaphoreType.DMA((2, n_col + owners)),
            pltpu.SemaphoreType.DMA((2, 2, n_z)),
            pltpu.SemaphoreType.DMA((2, n_z + owners)),
            pltpu.SemaphoreType.DMA((2, n_z + n_row)),
            pltpu.SemaphoreType.DMA((6,)),
        ],
        compiler_params=pltpu.CompilerParams(
            collective_id=0, has_side_effects=True, vmem_limit_bytes=58 * 1024 * 1024
        ),
    )(tile_rows, tile_cols, tile_count, bounds, tiles, vectors)


def solution(mesh):
    in_specs = (
        P(("row", "col"), None, None),
        P(("row", "col")),
        P(("row", "col")),
        P(("row", "col")),
        P(),
        P(("row", "col"), None),
    )
    out_specs = (P(("row", "col"), None), P())
    return jax.shard_map(
        functools.partial(on_device, mesh.shape["row"], mesh.shape["col"]),
        mesh=mesh,
        in_specs=in_specs,
        out_specs=out_specs,
        check_vma=False,
    )
```

```python
import functools

import jax
import jax.numpy as jnp
from jax import lax
from jax.experimental import pallas as pl
from jax.experimental.pallas import tpu as pltpu
from jax.sharding import PartitionSpec as P

BLK_COL = 2
UNROLL = 8
MESH = pl.DeviceIdType.MESH


def body(
    n_row,
    n_col,
    rows_any,
    cols_any,
    count_any,
    bounds_any,
    tiles_any,
    vectors_any,
    out,
    tile_rows,
    tile_cols,
    tile_count,
    bounds,
    tiles,
    vectors,
    panel_h,
    panel_t,
    piece,
    panel,
    fwd,
    bwd,
    swapped,
    fwd_send,
    bwd_send,
    landed,
    current,
    gram_part,
    gram_half,
    gram_z,
    gram_xy,
    in_sems,
    ga_send,
    ga_recv,
    swap_sems,
    sc_send,
    sc_recv,
    gram_sems,
):
    slots, size, _ = tiles_any.shape
    share, width = vectors.shape
    filtered = out.at[pl.ds(0, share)]
    gram = out.at[pl.ds(share, width)]
    n_z = n_col // 2
    ratio = n_col // n_row
    group = share * n_col
    blocks = group // size
    column = BLK_COL * size
    owners = column // share
    pairs = size // (2 * share)
    n_dev = n_row * n_col
    row, col = lax.axis_index("row"), lax.axis_index("col")
    core = lax.rem(col, 2)
    zed = col // 2
    sibling = zed * 2 + 1 - core
    live = row * ratio <= col
    diagonal = row == col // ratio
    first_z = row * ratio // 2
    column_of_mine = row * ratio + col // owners
    place_in_column = lax.rem(col, owners)
    part_of_column = lax.rem(col, ratio)
    column_base = jnp.where(diagonal, part_of_column * owners, n_col)

    def loop(count, step):
        def run(i, carry):
            step(i)
            return carry

        if count <= UNROLL:
            for i in range(count):
                step(i)
        else:
            lax.fori_loop(0, count, run, 0)

    def when(condition, action):
        pl.when(condition)(action)

    def far_first(i):
        return jnp.where(zed < n_z // 2, n_z - 1 - i, i)

    def near_first(i):
        return jnp.where(zed < n_z // 2, i, n_z - 1 - i)

    def when_not(value, mine, action):
        @pl.when(value != mine)
        def _():
            action()

    inputs = [
        pltpu.make_async_copy(vectors_any, vectors, in_sems.at[0]),
        pltpu.make_async_copy(tiles_any, tiles.at[pl.ds(0, slots)], in_sems.at[1]),
        pltpu.make_async_copy(rows_any, tile_rows, in_sems.at[2]),
        pltpu.make_async_copy(cols_any, tile_cols, in_sems.at[3]),
        pltpu.make_async_copy(count_any, tile_count, in_sems.at[4]),
        pltpu.make_async_copy(bounds_any, bounds, in_sems.at[5]),
    ]
    for copy in inputs:
        copy.start()

    barrier = pltpu.get_barrier_semaphore()

    def greet(other_row, other_col):
        pl.semaphore_signal(
            barrier, inc=1, device_id=(other_row, other_col), device_id_type=MESH
        )

    greet(row, sibling)
    loop(n_z, lambda z: when_not(z, zed, lambda: greet(row, z * 2 + core)))
    loop(n_row, lambda i: when_not(i, row, lambda: greet(i, col)))
    loop(n_row, lambda i: when_not(i, row, lambda: greet(i, sibling)))
    loop(n_row, lambda i: when(i < row, lambda: greet(i, column_of_mine)))
    across = live & jnp.logical_not(diagonal)

    @pl.when(across)
    def _():
        loop(owners, lambda j: greet(col // ratio, part_of_column * owners + j))

    inputs[0].wait()
    piece[0] = vectors[...].astype(jnp.bfloat16)
    tiles[slots] = jnp.zeros((size, size), jnp.bfloat16)
    pl.semaphore_wait(
        barrier, n_z + 2 * (n_row - 1) + row + jnp.where(across, owners, 0)
    )

    def remote(src, dst, send, recv, other_row, other_col):
        return pltpu.make_async_remote_copy(
            src_ref=src,
            dst_ref=dst,
            send_sem=send,
            recv_sem=recv,
            device_id=(other_row, other_col),
            device_id_type=MESH,
        )

    def gather_row(k, z):
        other = z * 2 + core
        return remote(
            piece.at[k], panel.at[k, col], ga_send.at[k, other], ga_recv.at[k, col], row, other
        )

    def gather_pair(k, z):
        slot = z * 2 + core
        return remote(
            panel.at[k, slot],
            panel.at[k, slot],
            ga_send.at[k, z * 2 + 1 - core],
            ga_recv.at[k, slot],
            row,
            sibling,
        )

    def gather_column(k, other):
        slot = n_col + place_in_column
        return remote(
            piece.at[k],
            panel.at[k, slot],
            ga_send.at[k, n_col + other],
            ga_recv.at[k, slot],
            other,
            column_of_mine,
        )

    def gather_landed(k, slot):
        return remote(
            piece.at[k], panel.at[k, slot], ga_send.at[k, 0], ga_recv.at[k, slot], row, sibling
        )

    def swap(k, z):
        return remote(
            fwd.at[1 - core, z],
            swapped.at[k, z],
            swap_sems.at[k, 0, z],
            swap_sems.at[k, 1, z],
            row,
            sibling,
        )

    def scatter_row(k, z):
        return remote(
            fwd_send.at[k, z],
            landed.at[k, zed],
            sc_send.at[k, z],
            sc_recv.at[k, zed],
            row,
            z * 2 + core,
        )

    def scatter_column(k, j):
        return remote(
            bwd_send.at[k, lax.rem(j, 2), j // 2],
            landed.at[k, n_z + row],
            sc_send.at[k, n_z + j],
            sc_recv.at[k, n_z + row],
            col // ratio,
            part_of_column * owners + j,
        )

    def scatter_landed(k, slot):
        return remote(
            piece.at[k], landed.at[k, slot], sc_send.at[k, 0], sc_recv.at[k, slot], row, sibling
        )

    def start_gather(k):
        @pl.when(live)
        def _():
            panel[k, col] = piece[k]

        def to_row(i):
            z = far_first(i)
            when((z >= first_z) & (z != zed), lambda: gather_row(k, z).start())

        loop(n_z, to_row)
        loop(n_row, lambda i: when(i < row, lambda: gather_column(k, i).start()))
        when(live, lambda: gather_pair(k, zed).start())

    def arrange():
        for i in range(blocks):
            for j in range(BLK_COL):
                slot = jnp.int32(slots)
                for s in range(slots):
                    here = (tile_rows[s] == i) & (tile_cols[s] == j) & (s < tile_count[0])
                    slot = jnp.where(here, jnp.int32(s), slot)
                block = tiles[slot]
                panel_h[pl.ds(i * size, size), pl.ds(j * size, size)] = block
                panel_t[pl.ds(j * size, size), pl.ds(i * size, size)] = block.T

    def forward_pair(k, z):
        gather_landed(k, z * 2 + core).wait_recv()
        gather_pair(k, z).start()

    def backward(k):
        rows_in = panel[k, pl.ds(0, n_col)].reshape(group, width)
        for j in range(BLK_COL):
            part = jnp.dot(
                panel_t[pl.ds(j * size, size)], rows_in, preferred_element_type=jnp.float32
            ).reshape(pairs, 2, share, width)
            for half in range(2):
                bwd[half, pl.ds(j * pairs, pairs)] = part[:, half]

    def products(k):
        def forward(i):
            z = near_first(i)
            when_not(z, zed, lambda: forward_pair(k, z))

        def rest_of_row():
            loop(n_z, lambda z: gather_landed(k, z * 2 + 1 - core).wait_recv())

        loop(n_z, forward)

        @pl.when(across)
        def _():
            loop(owners, lambda j: gather_landed(k, n_col + j).wait_recv())

        @pl.when(diagonal)
        def _():
            rest_of_row()
            backward(k)

        cols_in = panel[k, pl.ds(column_base, owners)].reshape(column, width)
        for i in range(blocks):
            part = jnp.dot(
                panel_h[pl.ds(i * size, size)], cols_in, preferred_element_type=jnp.float32
            ).reshape(pairs, 2, share, width)
            for half in range(2):
                fwd[half, pl.ds(i * pairs, pairs)] = part[:, half]

        @pl.when(diagonal)
        def _():
            here = pl.ds(part_of_column * (owners // 2), owners // 2)
            for half in range(2):
                fwd[half, here] += bwd[half]

        loop(n_z, lambda i: swap(k, far_first(i)).start())

        @pl.when(across)
        def _():
            rest_of_row()
            backward(k)
            bwd_send[k] = bwd[...].astype(jnp.bfloat16)
            loop(owners, lambda j: scatter_column(k, j).start())

        def send(i):
            z = far_first(i)
            swap(k, z).wait_recv()

            @pl.when(z != zed)
            def _():
                fwd_send[k, z] = (fwd[core, z] + swapped[k, z]).astype(jnp.bfloat16)
                scatter_row(k, z).start()

        loop(n_z, send)
        filtered[...] = fwd[core, zed] + swapped[k, zed]
        loop(n_z, lambda z: swap(k, z).wait_send())

    def apply(k):
        if k == 0:
            for copy in inputs[1:]:
                copy.wait()

        @pl.when(live)
        def _():
            if k == 0:
                arrange()
            products(k)

        @pl.when(jnp.logical_not(live))
        def _():
            filtered[...] = jnp.zeros_like(filtered)

        def add(slot):
            scatter_landed(k, slot).wait_recv()
            filtered[...] += landed[k, slot].astype(jnp.float32)

        def add_row(i):
            z = near_first(i)
            when((z >= first_z) & (z != zed), lambda: add(z))

        loop(n_z, add_row)
        loop(n_row, lambda i: when(i < row, lambda: add(n_z + i)))
        return filtered[...]

    def finish_sends(k):
        def sent(z):
            when((z >= first_z) & (z != zed), lambda: gather_row(k, z).wait_send())

        loop(n_z, sent)
        loop(n_row, lambda i: when(i < row, lambda: gather_column(k, i).wait_send()))

        @pl.when(live)
        def _():
            loop(n_z, lambda z: gather_pair(k, z).wait_send())
            loop(n_z, lambda z: when_not(z, zed, lambda: scatter_row(k, z).wait_send()))

        @pl.when(across)
        def _():
            loop(owners, lambda j: scatter_column(k, j).wait_send())

    start_gather(0)
    image = apply(0)
    center = (bounds[1] + bounds[0]) * 0.5
    halfwidth = (bounds[1] - bounds[0]) * 0.5
    first = (image - center * vectors[...]) / halfwidth
    current[...] = first
    piece[1] = first.astype(jnp.bfloat16)
    start_gather(1)
    image = apply(1)
    last = 2.0 * (image - center * current[...]) / halfwidth - vectors[...]
    filtered[...] = last

    part = lax.dot_general(
        last,
        last,
        (((0,), (0,)), ((), ())),
        precision=lax.Precision.HIGHEST,
        preferred_element_type=jnp.float32,
    )
    height = width // 2
    gram_part[...] = part.reshape(2, height, width)

    def gram_swap():
        return remote(
            gram_part.at[1 - core], gram_half, gram_sems.at[0], gram_sems.at[1], row, sibling
        )

    def gram_row(z):
        return remote(
            gram_z.at[zed],
            gram_z.at[zed],
            gram_sems.at[2],
            gram_sems.at[3],
            row,
            z * 2 + core,
        )

    def gram_out(i, other):
        here = core * n_row + row
        return remote(
            gram_xy.at[here], gram_xy.at[here], gram_sems.at[4], gram_sems.at[5], i, other
        )

    def wait_bytes(ref, sem):
        pltpu.make_async_copy(ref, ref, gram_sems.at[sem]).wait()

    gram_swap().start()
    finish_sends(0)
    gram_swap().wait_recv()
    gram_z[zed] = (gram_part[core] + gram_half[...]).astype(jnp.bfloat16)

    def to_row(i):
        z = far_first(i)
        when_not(z, zed, lambda: gram_row(z).start())

    loop(n_z, to_row)
    finish_sends(1)
    gram_swap().wait_send()
    wait_bytes(gram_z.at[pl.ds(0, n_z - 1)], 3)
    gram_xy[core * n_row + row] = jnp.sum(gram_z[...].astype(jnp.float32), axis=0).astype(
        jnp.bfloat16
    )
    loop(n_row, lambda i: when_not(i, row, lambda: gram_out(i, col).start()))
    loop(n_row, lambda i: when_not(i, row, lambda: gram_out(i, sibling).start()))
    gram_out(row, sibling).start()
    wait_bytes(gram_z.at[pl.ds(0, n_z - 1)], 2)
    wait_bytes(gram_xy.at[pl.ds(0, 2 * n_row - 1)], 5)
    for half in range(2):
        total = jnp.sum(gram_xy[pl.ds(half * n_row, n_row)].astype(jnp.float32), axis=0)
        gram[pl.ds(half * height, height)] = total / (share * n_dev)
    wait_bytes(gram_xy.at[pl.ds(0, 2 * n_row - 1)], 4)


def on_device(n_row, n_col, tiles, tile_rows, tile_cols, tile_count, bounds, vectors):
    slots, size, _ = tiles.shape
    share, width = vectors.shape
    n_z = n_col // 2
    group = share * n_col
    column = BLK_COL * size
    owners = column // share
    height = width // 2
    hbm = pl.BlockSpec(memory_space=pl.ANY)
    vmem = pl.BlockSpec(memory_space=pltpu.VMEM)
    half, full = jnp.bfloat16, jnp.float32
    both = pl.pallas_call(
        functools.partial(body, n_row, n_col),
        out_shape=jax.ShapeDtypeStruct((share + width, width), full),
        in_specs=[pl.BlockSpec(memory_space=pltpu.HBM)] * 6,
        out_specs=vmem,
        scratch_shapes=[
            pltpu.SMEM((slots,), jnp.int32),
            pltpu.SMEM((slots,), jnp.int32),
            pltpu.SMEM((1,), jnp.int32),
            pltpu.SMEM((2,), full),
            pltpu.VMEM((slots + 1, size, size), half),
            pltpu.VMEM((share, width), full),
            pltpu.VMEM((group, column), half),
            pltpu.VMEM((column, group), half),
            pltpu.VMEM((2, share, width), half),
            pltpu.VMEM((2, n_col + owners, share, width), half),
            pltpu.VMEM((2, n_z, share, width), full),
            pltpu.VMEM((2, owners // 2, share, width), full),
            pltpu.VMEM((2, n_z, share, width), full),
            pltpu.VMEM((2, n_z, share, width), half),
            pltpu.VMEM((2, 2, owners // 2, share, width), half),
            pltpu.VMEM((2, n_z + n_row, share, width), half),
            pltpu.VMEM((share, width), full),
            pltpu.VMEM((2, height, width), full),
            pltpu.VMEM((height, width), full),
            pltpu.VMEM((n_z, height, width), half),
            pltpu.VMEM((2 * n_row, height, width), half),
            pltpu.SemaphoreType.DMA((6,)),
            pltpu.SemaphoreType.DMA((2, n_col + n_row)),
            pltpu.SemaphoreType.DMA((2, n_col + owners)),
            pltpu.SemaphoreType.DMA((2, 2, n_z)),
            pltpu.SemaphoreType.DMA((2, n_z + owners)),
            pltpu.SemaphoreType.DMA((2, n_z + n_row)),
            pltpu.SemaphoreType.DMA((6,)),
        ],
        compiler_params=pltpu.CompilerParams(
            collective_id=0, has_side_effects=True, vmem_limit_bytes=58 * 1024 * 1024
        ),
    )(tile_rows, tile_cols, tile_count, bounds, tiles, vectors)
    return both[:share], both[share:]


def solution(mesh):
    in_specs = (
        P(("row", "col"), None, None),
        P(("row", "col")),
        P(("row", "col")),
        P(("row", "col")),
        P(),
        P(("row", "col"), None),
    )
    out_specs = (P(("row", "col"), None), P())
    return jax.shard_map(
        functools.partial(on_device, mesh.shape["row"], mesh.shape["col"]),
        mesh=mesh,
        in_specs=in_specs,
        out_specs=out_specs,
        check_vma=False,
    )
```

```python
import functools

import jax
import jax.numpy as jnp
from jax import lax
from jax.experimental import pallas as pl
from jax.experimental.pallas import tpu as pltpu
from jax.sharding import PartitionSpec as P

BLK_COL = 2
UNROLL = 8
MESH = pl.DeviceIdType.MESH


def body(
    n_row,
    n_col,
    rows_any,
    cols_any,
    count_any,
    bounds_any,
    tiles_any,
    vectors_any,
    out,
    tile_rows,
    tile_cols,
    tile_count,
    bounds,
    tiles,
    vectors,
    panel_h,
    panel_t,
    piece,
    panel,
    fwd,
    bwd,
    swapped,
    fwd_send,
    bwd_send,
    landed,
    current,
    gram_part,
    gram_half,
    gram_z,
    gram_xy,
    in_sems,
    ga_send,
    ga_recv,
    swap_sems,
    sc_send,
    sc_recv,
    gram_sems,
):
    slots, size, _ = tiles_any.shape
    share, width = vectors.shape
    filtered = out.at[pl.ds(0, share)]
    gram = out.at[pl.ds(share, width)]
    n_z = n_col // 2
    ratio = n_col // n_row
    group = share * n_col
    blocks = group // size
    column = BLK_COL * size
    owners = column // share
    pairs = size // (2 * share)
    n_dev = n_row * n_col
    row, col = lax.axis_index("row"), lax.axis_index("col")
    core = lax.rem(col, 2)
    zed = col // 2
    sibling = zed * 2 + 1 - core
    live = row * ratio <= col
    diagonal = row == col // ratio
    first_z = row * ratio // 2
    column_of_mine = row * ratio + col // owners
    place_in_column = lax.rem(col, owners)
    part_of_column = lax.rem(col, ratio)
    column_base = jnp.where(diagonal, part_of_column * owners, n_col)

    def loop(count, step):
        def run(i, carry):
            step(i)
            return carry

        if count <= UNROLL:
            for i in range(count):
                step(i)
        else:
            lax.fori_loop(0, count, run, 0)

    def when(condition, action):
        pl.when(condition)(action)

    def far_first(i):
        return jnp.where(zed < n_z // 2, n_z - 1 - i, i)

    def near_first(i):
        return jnp.where(zed < n_z // 2, i, n_z - 1 - i)

    def when_not(value, mine, action):
        @pl.when(value != mine)
        def _():
            action()

    inputs = [
        pltpu.make_async_copy(vectors_any, vectors, in_sems.at[0]),
        pltpu.make_async_copy(tiles_any, tiles.at[pl.ds(0, slots)], in_sems.at[1]),
        pltpu.make_async_copy(rows_any, tile_rows, in_sems.at[2]),
        pltpu.make_async_copy(cols_any, tile_cols, in_sems.at[3]),
        pltpu.make_async_copy(count_any, tile_count, in_sems.at[4]),
        pltpu.make_async_copy(bounds_any, bounds, in_sems.at[5]),
    ]
    for copy in inputs:
        copy.start()

    barrier = pltpu.get_barrier_semaphore()

    def greet(other_row, other_col):
        pl.semaphore_signal(
            barrier, inc=1, device_id=(other_row, other_col), device_id_type=MESH
        )

    across = live & jnp.logical_not(diagonal)

    def greet_row(i):
        z = far_first(i)
        when_not(z, zed, lambda: greet(row, z * 2 + core))

    loop(n_z, greet_row)
    loop(n_row, lambda i: when(i < row, lambda: greet(i, column_of_mine)))

    @pl.when(across)
    def _():
        loop(owners, lambda j: greet(col // ratio, part_of_column * owners + j))

    loop(n_row, lambda i: when_not(i, row, lambda: greet(i, col)))
    loop(n_row, lambda i: when_not(i, row, lambda: greet(i, sibling)))
    greet(row, sibling)
    inputs[0].wait()
    piece[0] = vectors[...].astype(jnp.bfloat16)
    tiles[slots] = jnp.zeros((size, size), jnp.bfloat16)
    pl.semaphore_wait(
        barrier, n_z + 2 * (n_row - 1) + row + jnp.where(across, owners, 0)
    )

    def remote(src, dst, send, recv, other_row, other_col):
        return pltpu.make_async_remote_copy(
            src_ref=src,
            dst_ref=dst,
            send_sem=send,
            recv_sem=recv,
            device_id=(other_row, other_col),
            device_id_type=MESH,
        )

    def gather_row(k, z):
        other = z * 2 + core
        return remote(
            piece.at[k], panel.at[k, col], ga_send.at[k, other], ga_recv.at[k, col], row, other
        )

    def gather_pair(k, z):
        slot = z * 2 + core
        return remote(
            panel.at[k, slot],
            panel.at[k, slot],
            ga_send.at[k, z * 2 + 1 - core],
            ga_recv.at[k, slot],
            row,
            sibling,
        )

    def gather_column(k, other):
        slot = n_col + place_in_column
        return remote(
            piece.at[k],
            panel.at[k, slot],
            ga_send.at[k, n_col + other],
            ga_recv.at[k, slot],
            other,
            column_of_mine,
        )

    def gather_landed(k, slot):
        return remote(
            piece.at[k], panel.at[k, slot], ga_send.at[k, 0], ga_recv.at[k, slot], row, sibling
        )

    def swap(k, z):
        return remote(
            fwd.at[1 - core, z],
            swapped.at[k, z],
            swap_sems.at[k, 0, z],
            swap_sems.at[k, 1, z],
            row,
            sibling,
        )

    def scatter_row(k, z):
        return remote(
            fwd_send.at[k, z],
            landed.at[k, zed],
            sc_send.at[k, z],
            sc_recv.at[k, zed],
            row,
            z * 2 + core,
        )

    def scatter_column(k, j):
        return remote(
            bwd_send.at[k, lax.rem(j, 2), j // 2],
            landed.at[k, n_z + row],
            sc_send.at[k, n_z + j],
            sc_recv.at[k, n_z + row],
            col // ratio,
            part_of_column * owners + j,
        )

    def scatter_landed(k, slot):
        return remote(
            piece.at[k], landed.at[k, slot], sc_send.at[k, 0], sc_recv.at[k, slot], row, sibling
        )

    def start_gather(k):
        @pl.when(live)
        def _():
            panel[k, col] = piece[k]

        def to_row(i):
            z = far_first(i)
            when((z >= first_z) & (z != zed), lambda: gather_row(k, z).start())

        loop(n_z, to_row)
        loop(n_row, lambda i: when(i < row, lambda: gather_column(k, i).start()))
        when(live, lambda: gather_pair(k, zed).start())

    def arrange():
        for i in range(blocks):
            for j in range(BLK_COL):
                slot = jnp.int32(slots)
                for s in range(slots):
                    here = (tile_rows[s] == i) & (tile_cols[s] == j) & (s < tile_count[0])
                    slot = jnp.where(here, jnp.int32(s), slot)
                block = tiles[slot]
                panel_h[pl.ds(i * size, size), pl.ds(j * size, size)] = block
                panel_t[pl.ds(j * size, size), pl.ds(i * size, size)] = block.T

    def forward_pair(k, z):
        gather_landed(k, z * 2 + core).wait_recv()
        gather_pair(k, z).start()

    def backward(k):
        rows_in = panel[k, pl.ds(0, n_col)].reshape(group, width)
        for j in range(BLK_COL):
            part = jnp.dot(
                panel_t[pl.ds(j * size, size)], rows_in, preferred_element_type=jnp.float32
            ).reshape(pairs, 2, share, width)
            for half in range(2):
                bwd[half, pl.ds(j * pairs, pairs)] = part[:, half]

    def products(k):
        def forward(i):
            z = near_first(i)
            when_not(z, zed, lambda: forward_pair(k, z))

        def rest_of_row():
            loop(n_z, lambda z: gather_landed(k, z * 2 + 1 - core).wait_recv())

        loop(n_z, forward)

        @pl.when(across)
        def _():
            loop(owners, lambda j: gather_landed(k, n_col + j).wait_recv())

        @pl.when(diagonal)
        def _():
            rest_of_row()
            backward(k)

        cols_in = panel[k, pl.ds(column_base, owners)].reshape(column, width)
        for i in range(blocks):
            part = jnp.dot(
                panel_h[pl.ds(i * size, size)], cols_in, preferred_element_type=jnp.float32
            ).reshape(pairs, 2, share, width)
            for half in range(2):
                fwd[half, pl.ds(i * pairs, pairs)] = part[:, half]

        @pl.when(diagonal)
        def _():
            here = pl.ds(part_of_column * (owners // 2), owners // 2)
            for half in range(2):
                fwd[half, here] += bwd[half]

        loop(n_z, lambda i: swap(k, far_first(i)).start())

        @pl.when(across)
        def _():
            rest_of_row()
            backward(k)
            bwd_send[k] = bwd[...].astype(jnp.bfloat16)
            loop(owners, lambda j: scatter_column(k, j).start())

        def send(i):
            z = far_first(i)
            swap(k, z).wait_recv()

            @pl.when(z != zed)
            def _():
                fwd_send[k, z] = (fwd[core, z] + swapped[k, z]).astype(jnp.bfloat16)
                scatter_row(k, z).start()

        loop(n_z, send)
        filtered[...] = fwd[core, zed] + swapped[k, zed]
        loop(n_z, lambda z: swap(k, z).wait_send())

    def apply(k):
        if k == 0:
            for copy in inputs[1:]:
                copy.wait()

        @pl.when(live)
        def _():
            if k == 0:
                arrange()
            products(k)

        @pl.when(jnp.logical_not(live))
        def _():
            filtered[...] = jnp.zeros_like(filtered)

        def add(slot):
            scatter_landed(k, slot).wait_recv()
            filtered[...] += landed[k, slot].astype(jnp.float32)

        def add_row(i):
            z = near_first(i)
            when((z >= first_z) & (z != zed), lambda: add(z))

        loop(n_z, add_row)
        loop(n_row, lambda i: when(i < row, lambda: add(n_z + i)))
        return filtered[...]

    def finish_sends(k):
        def sent(z):
            when((z >= first_z) & (z != zed), lambda: gather_row(k, z).wait_send())

        loop(n_z, sent)
        loop(n_row, lambda i: when(i < row, lambda: gather_column(k, i).wait_send()))

        @pl.when(live)
        def _():
            loop(n_z, lambda z: gather_pair(k, z).wait_send())
            loop(n_z, lambda z: when_not(z, zed, lambda: scatter_row(k, z).wait_send()))

        @pl.when(across)
        def _():
            loop(owners, lambda j: scatter_column(k, j).wait_send())

    start_gather(0)
    image = apply(0)
    center = (bounds[1] + bounds[0]) * 0.5
    halfwidth = (bounds[1] - bounds[0]) * 0.5
    first = (image - center * vectors[...]) / halfwidth
    current[...] = first
    piece[1] = first.astype(jnp.bfloat16)
    start_gather(1)
    image = apply(1)
    last = 2.0 * (image - center * current[...]) / halfwidth - vectors[...]
    filtered[...] = last

    part = lax.dot_general(
        last,
        last,
        (((0,), (0,)), ((), ())),
        precision=lax.Precision.HIGHEST,
        preferred_element_type=jnp.float32,
    )
    height = width // 2
    gram_part[...] = part.reshape(2, height, width)

    def gram_swap():
        return remote(
            gram_part.at[1 - core], gram_half, gram_sems.at[0], gram_sems.at[1], row, sibling
        )

    def gram_row(z):
        return remote(
            gram_z.at[zed],
            gram_z.at[zed],
            gram_sems.at[2],
            gram_sems.at[3],
            row,
            z * 2 + core,
        )

    def gram_out(i, other):
        here = core * n_row + row
        return remote(
            gram_xy.at[here], gram_xy.at[here], gram_sems.at[4], gram_sems.at[5], i, other
        )

    def wait_bytes(ref, sem):
        pltpu.make_async_copy(ref, ref, gram_sems.at[sem]).wait()

    gram_swap().start()
    finish_sends(0)
    gram_swap().wait_recv()
    gram_z[zed] = (gram_part[core] + gram_half[...]).astype(jnp.bfloat16)

    def to_row(i):
        z = far_first(i)
        when_not(z, zed, lambda: gram_row(z).start())

    loop(n_z, to_row)
    finish_sends(1)
    gram_swap().wait_send()
    wait_bytes(gram_z.at[pl.ds(0, n_z - 1)], 3)
    gram_xy[core * n_row + row] = jnp.sum(gram_z[...].astype(jnp.float32), axis=0).astype(
        jnp.bfloat16
    )
    loop(n_row, lambda i: when_not(i, row, lambda: gram_out(i, col).start()))
    loop(n_row, lambda i: when_not(i, row, lambda: gram_out(i, sibling).start()))
    gram_out(row, sibling).start()
    wait_bytes(gram_z.at[pl.ds(0, n_z - 1)], 2)
    wait_bytes(gram_xy.at[pl.ds(0, 2 * n_row - 1)], 5)
    for half in range(2):
        total = jnp.sum(gram_xy[pl.ds(half * n_row, n_row)].astype(jnp.float32), axis=0)
        gram[pl.ds(half * height, height)] = total / (share * n_dev)
    wait_bytes(gram_xy.at[pl.ds(0, 2 * n_row - 1)], 4)


def on_device(n_row, n_col, tiles, tile_rows, tile_cols, tile_count, bounds, vectors):
    slots, size, _ = tiles.shape
    share, width = vectors.shape
    n_z = n_col // 2
    group = share * n_col
    column = BLK_COL * size
    owners = column // share
    height = width // 2
    hbm = pl.BlockSpec(memory_space=pl.ANY)
    vmem = pl.BlockSpec(memory_space=pltpu.VMEM)
    half, full = jnp.bfloat16, jnp.float32
    both = pl.pallas_call(
        functools.partial(body, n_row, n_col),
        out_shape=jax.ShapeDtypeStruct((share + width, width), full),
        in_specs=[pl.BlockSpec(memory_space=pltpu.HBM)] * 6,
        out_specs=vmem,
        scratch_shapes=[
            pltpu.SMEM((slots,), jnp.int32),
            pltpu.SMEM((slots,), jnp.int32),
            pltpu.SMEM((1,), jnp.int32),
            pltpu.SMEM((2,), full),
            pltpu.VMEM((slots + 1, size, size), half),
            pltpu.VMEM((share, width), full),
            pltpu.VMEM((group, column), half),
            pltpu.VMEM((column, group), half),
            pltpu.VMEM((2, share, width), half),
            pltpu.VMEM((2, n_col + owners, share, width), half),
            pltpu.VMEM((2, n_z, share, width), full),
            pltpu.VMEM((2, owners // 2, share, width), full),
            pltpu.VMEM((2, n_z, share, width), full),
            pltpu.VMEM((2, n_z, share, width), half),
            pltpu.VMEM((2, 2, owners // 2, share, width), half),
            pltpu.VMEM((2, n_z + n_row, share, width), half),
            pltpu.VMEM((share, width), full),
            pltpu.VMEM((2, height, width), full),
            pltpu.VMEM((height, width), full),
            pltpu.VMEM((n_z, height, width), half),
            pltpu.VMEM((2 * n_row, height, width), half),
            pltpu.SemaphoreType.DMA((6,)),
            pltpu.SemaphoreType.DMA((2, n_col + n_row)),
            pltpu.SemaphoreType.DMA((2, n_col + owners)),
            pltpu.SemaphoreType.DMA((2, 2, n_z)),
            pltpu.SemaphoreType.DMA((2, n_z + owners)),
            pltpu.SemaphoreType.DMA((2, n_z + n_row)),
            pltpu.SemaphoreType.DMA((6,)),
        ],
        compiler_params=pltpu.CompilerParams(
            collective_id=0, has_side_effects=True, vmem_limit_bytes=58 * 1024 * 1024
        ),
    )(tile_rows, tile_cols, tile_count, bounds, tiles, vectors)
    return both[:share], both[share:]


def solution(mesh):
    in_specs = (
        P(("row", "col"), None, None),
        P(("row", "col")),
        P(("row", "col")),
        P(("row", "col")),
        P(),
        P(("row", "col"), None),
    )
    out_specs = (P(("row", "col"), None), P())
    return jax.shard_map(
        functools.partial(on_device, mesh.shape["row"], mesh.shape["col"]),
        mesh=mesh,
        in_specs=in_specs,
        out_specs=out_specs,
        check_vma=False,
    )
```
